1024 devices in a mesh: gx: 32 (over z), gy: 4 (over y), gz: 8 (over x, core).
Axes of the slice: x: 4, y: 4, z: 32, core: 2. Of those that a mesh axis runs over, the one named last changes fastest.
Arguments:
- bands: bfloat16 [64, 128, 64, 1024], P(None, 'gx', 'gy', 'gz'), may hold values from -48 to 48
- potential: float32 [128, 64, 1024], P('gx', 'gy', 'gz'), may hold values from -3 to 0
- coupling: float32 [2048], replicated, may hold values from 0.5 to 2
- proj_atom: int32 [1024, 256], P(('gx', 'gy', 'gz')), may hold values from 0 to 2047, as said below
- proj_cell: int32 [1024, 256], P(('gx', 'gy', 'gz')), may hold values from 0 to 8191
- proj_value: float32 [1024, 256], P(('gx', 'gy', 'gz')), may hold values from -1 to 1
Outputs:
- filtered: bfloat16 [64, 128, 64, 1024], P(None, 'gx', 'gy', 'gz')
- gram: float32 [64, 64], replicated
The draws below stay inside these ranges and needn't reach their ends.
Inputs may be any that keep to these rules, and one draw needn't show every extreme that they name: `proj_atom`: every point listed in row d names an atom whose owning device block differs from d's block by at most one along each of gx, gy and gz.
All inputs are finite; a program needn't handle non-finite values.
Results may differ from the reference program's by a relative error of at most 0.00065.
The reference program's roundings to bfloat16 on the way count: a program that leaves them out, or rounds other values in their place, can miss the bound.
Values may be sent and summed in bfloat16 or wider, within the bound.
A program may use at most 64 MiB of HBM per device.

```python
import math
import jax
import jax.numpy as jnp
from jax import lax

BANDS = 64
CX = 4
CY = 16
CZ = 128
A_DEV = 2
ENTRIES = 256
DEGREE = 3
NX = 128
NY = 64
NZ = 1024
ATOMS = 2048
N_GX = 32
N_GY = 4
N_GZ = 8
DEVICES = 1024


def draw_bands(key, part):
    key = jax.random.fold_in(key, 5)
    base_key, band_key, plane_key = jax.random.split(key, 3)
    shape = (BANDS, NX, NY, NZ)
    band_scale = jnp.exp(jax.random.uniform(band_key, (BANDS, 1, 1, 1), jnp.float32, math.log(0.3), math.log(3.0)))
    plane_scale = jnp.exp(jax.random.uniform(plane_key, (1, NX, 1, 1), jnp.float32, math.log(0.3), math.log(3.0)))
    position = jnp.arange(NX, dtype=jnp.float32).reshape(1, NX, 1, 1) / NX
    base = jax.random.truncated_normal(base_key, -3.5, 3.5, shape, jnp.float32)
    ramp = 0.5 + position
    return (base * band_scale * plane_scale * ramp).astype(jnp.bfloat16)


def draw_proj_atom(key, part):
    key = jax.random.fold_in(key, 11)
    offset_key, slot_key = jax.random.split(key)
    device = jnp.arange(DEVICES, dtype=jnp.int32)[:, None]
    index_x = device // (N_GY * N_GZ)
    index_y = device // N_GZ % N_GY
    index_z = device % N_GZ
    offsets = jax.random.randint(offset_key, (3, DEVICES, ENTRIES), -1, 2)
    owner_x = jnp.clip(index_x + offsets[0], 0, N_GX - 1)
    owner_y = jnp.clip(index_y + offsets[1], 0, N_GY - 1)
    owner_z = jnp.clip(index_z + offsets[2], 0, N_GZ - 1)
    slots = jax.random.randint(slot_key, (DEVICES, ENTRIES), 0, A_DEV)
    owner = (owner_x * N_GY + owner_y) * N_GZ + owner_z
    return (owner * A_DEV + slots).astype(jnp.int32)


def set_ends(array, own_key, least, top_value):
    extent = array.shape
    spot = [jax.random.randint(jax.random.fold_in(own_key, axis), (), 0, extent[axis]) for axis in range(len(extent))]
    array = array.at[tuple(spot)].set(least)
    longest = extent.index(max(extent))
    spot[longest] = (spot[longest] + 1) % extent[longest]
    return array.at[tuple(spot)].set(top_value)


def steps_of(key, extent, pieces, smallest, largest):
    loudness, own = 1.0, jax.random.fold_in(key, 6)
    for axis_at, blocks in pieces:
        draws = jnp.exp(jax.random.uniform(jax.random.fold_in(own, axis_at), (blocks,), jnp.float32, smallest / len(pieces), largest / len(pieces)))
        loudness = loudness * jnp.repeat(draws, extent[axis_at] // blocks).reshape([-1 if axis == axis_at else 1 for axis in range(len(extent))])
    return loudness


def centred(rng, extent, spread, limit, shards=(), held_as=jnp.bfloat16):
    gain = steps_of(rng, extent, shards, -0.22, 0.18) if shards else 1.0
    result = jax.random.normal(rng, extent, jnp.float32) * spread * gain
    return jnp.minimum(jnp.maximum(result, -limit), limit).astype(held_as)


def setup_inputs(seed: int = 0) -> dict:
    seeds = jax.random.split(jax.random.key(seed), 7)
    return {
        "bands": draw_bands(jax.random.fold_in(seeds[6], 71), 0),
        "potential": jnp.clip(-3.0 + 3.0 * jax.random.uniform(seeds[1], (NX, NY, NZ), jnp.float32) ** steps_of(seeds[1], (NX, NY, NZ), ((0, 32), (1, 4), (2, 8)), -0.2, 0.2), -3.0, 0.0),
        "coupling": jnp.clip(jnp.exp(jax.random.uniform(seeds[2], (ATOMS,), jnp.float32, math.log(0.5), math.log(2.0))), 0.5, 2.0),
        "proj_atom": draw_proj_atom(jax.random.fold_in(seeds[6], 71), 0),
        "proj_cell": set_ends(jax.random.randint(seeds[4], (DEVICES, ENTRIES), 0, CX * CY * CZ), jax.random.fold_in(seeds[4], 1), 0, (CX * CY * CZ) - 1).astype(jnp.int32),
        "proj_value": centred(seeds[5], (DEVICES, ENTRIES), 0.25, 1.0, ((0, 1024),), jnp.float32),
    }


STENCIL = (-205.0 / 72.0, 8.0 / 5.0, -1.0 / 5.0, 8.0 / 315.0, -1.0 / 560.0)
FILTER_CENTRE = 8.25
FILTER_HALF = 7.75


def entry_cells(proj_cell):
    device = jnp.arange(DEVICES, dtype=jnp.int32)[:, None]
    index_x = device // (N_GY * N_GZ)
    index_y = (device // N_GZ) % N_GY
    index_z = device % N_GZ
    local_x = proj_cell // (CY * CZ)
    local_y = (proj_cell // CZ) % CY
    local_z = proj_cell % CZ
    whole = ((index_x * CX + local_x) * NY + index_y * CY + local_y) * NZ + index_z * CZ + local_z
    return whole.reshape(-1).astype(jnp.int32)


def axis_term(extended, dim, length):
    total = jnp.zeros_like(lax.slice_in_dim(extended, 4, 4 + length, axis=dim)).astype(jnp.float32)
    for offset in range(1, 5):
        upper = lax.slice_in_dim(extended, 4 + offset, 4 + offset + length, axis=dim).astype(jnp.float32)
        lower = lax.slice_in_dim(extended, 4 - offset, 4 - offset + length, axis=dim).astype(jnp.float32)
        total = total + STENCIL[offset] * (upper + lower)
    return total


def laplacian(field):
    total = 3.0 * STENCIL[0] * field
    for dim in (1, 2, 3):
        widths = [(0, 0)] * 4
        widths[dim] = (4, 4)
        total = total + axis_term(jnp.pad(field, widths), dim, field.shape[dim])
    return total


def apply_h(block, potential, coupling, atoms, cells, values):
    field = block.astype(jnp.float32)
    count = field.shape[0]
    flat = field.reshape(count, -1)
    picked = flat[:, cells] * values[None, :]
    partial_value = jax.ops.segment_sum(picked.T, atoms, num_segments=ATOMS)
    scaled = partial_value * coupling[:, None]
    back = (scaled[atoms] * values[:, None]).T
    projected = jnp.zeros_like(flat).at[:, cells].add(back)
    return -0.5 * laplacian(field) + potential[None] * field + projected.reshape(field.shape)


def reference(bands, potential, coupling, proj_atom, proj_cell, proj_value):
    atoms = proj_atom.reshape(-1).astype(jnp.int32)
    cells = entry_cells(proj_cell)
    values = proj_value.reshape(-1)

    def filter_block(block):
        previous = block
        image = apply_h(block, potential, coupling, atoms, cells, values)
        current = ((image - FILTER_CENTRE * block.astype(jnp.float32)) / FILTER_HALF).astype(jnp.bfloat16)
        for step in range(DEGREE - 1):
            image = apply_h(current, potential, coupling, atoms, cells, values)
            following = 2.0 * (image - FILTER_CENTRE * current.astype(jnp.float32)) / FILTER_HALF - previous.astype(jnp.float32)
            previous = current
            current = following.astype(jnp.bfloat16)
        return current

    grouped = bands.reshape(BANDS // 8, 8, NX, NY, NZ)
    filtered = lax.map(filter_block, grouped).reshape(BANDS, NX, NY, NZ)
    flat = filtered.reshape(BANDS, NX * NY * NZ)
    gram = jnp.dot(flat, flat.T, preferred_element_type=jnp.float32) / float(NX * NY * NZ)
    return filtered, gram
```

```python
import jax
import jax.numpy as jnp
import ml_dtypes
import numpy as np
from jax import lax
from jax.experimental import pallas as pl
from jax.experimental.pallas import tpu as pltpu
from jax.sharding import PartitionSpec as P

A_DEV = 2
DEGREE = 3
STENCIL = (-205.0 / 72.0, 8.0 / 5.0, -1.0 / 5.0, 8.0 / 315.0, -1.0 / 560.0)
FILTER_CENTRE = 8.25
FILTER_HALF = 7.75

GROUP = 16
KEYS = 64
SPAN = {}
STAGES = (("gz", 2), ("gy", 6), ("gx", 18), ("gx", 18), ("gy", 6), ("gz", 2))
OWN_LANE = 26
F32 = jnp.float32
BF16 = jnp.bfloat16


def beside(axis, offset):
    n = SPAN[axis]
    return {axis: lax.rem(lax.axis_index(axis) + offset + n, n)}


def split(value):
    high = value.astype(BF16)
    return high, (value - high.astype(F32)).astype(BF16)


def kernel(
    y0_ref, pot_ref, coup_ref, atom_ref, cell_ref, val_ref, wz_ref,
    out_ref, gram_ref,
    field, y_halo, z_pack, z_halo, gather_op, scatter_op, key_in, key_out, table, coup_row, potq,
    q_send, q_recv, q0_send, q0_recv,
    g_part, r_z, s_z, r_y, s_y, r_x, g_all,
    load_sem, out_sem, x_ss, x_rs, y_ss, y_rs, z_ss, z_rs, q_ss, q_rs, q0_ss, q0_rs,
    sz, rz, sy, ry, sx, rx,
):
    groups, size_x, size_y = field.shape[1], 4, field.shape[3]
    span_x, span_y, span_z = SPAN["gx"], SPAN["gy"], SPAN["gz"]
    here = {axis: lax.axis_index(axis) for axis in SPAN}
    first = {a: jnp.where(here[a] == 0, 0.0, 1.0).astype(F32) for a in SPAN}
    last = {a: jnp.where(here[a] == SPAN[a] - 1, 0.0, 1.0).astype(F32) for a in SPAN}

    def load_copy(g):
        return pltpu.make_async_copy(y0_ref.at[g], field.at[0, g, pl.ds(4, 4)], load_sem.at[g])

    def out_copy(g):
        return pltpu.make_async_copy(
            field.at[DEGREE, g, pl.ds(4, 4)], out_ref.at[g], out_sem.at[g]
        )

    def x_copy(k, g, x, side):
        return pltpu.make_async_remote_copy(
            field.at[k, g, 4 + x],
            field.at[k, g, x if side == 0 else 8 + x],
            x_ss.at[k, g, x, side],
            x_rs.at[k, g, x, side],
            device_id=beside("gx", 1 - 2 * side),
        )

    def y_copy(k, g, side):
        rows = pl.ds(12, 4) if side == 0 else pl.ds(0, 4)
        return pltpu.make_async_remote_copy(
            field.at[k, g, pl.ds(4, 4), rows],
            y_halo.at[k, g, side],
            y_ss.at[k, g, side],
            y_rs.at[k, g, side],
            device_id=beside("gy", 1 - 2 * side),
        )

    def z_copy(k, g, side):
        return pltpu.make_async_remote_copy(
            z_pack.at[k, g],
            z_halo.at[k, g, side],
            z_ss.at[k, g, side],
            z_rs.at[k, g, side],
            device_id=beside("gz", 1 - 2 * side),
        )

    def q_copy(chain, stage, side):
        return pltpu.make_async_remote_copy(
            q_send.at[chain, stage],
            q_recv.at[chain, stage, side],
            q_ss.at[chain, stage, side],
            q_rs.at[chain, stage, side],
            device_id=beside(STAGES[stage][0], 1 - 2 * side),
        )

    def q0_copy(stage, side):
        return pltpu.make_async_remote_copy(
            q0_send.at[stage],
            q0_recv.at[stage, side],
            q0_ss.at[stage, side],
            q0_rs.at[stage, side],
            device_id=beside(STAGES[stage][0], 1 - 2 * side),
        )

    for g in range(groups):
        load_copy(g).start()
    barrier = pltpu.get_barrier_semaphore()
    partners = [(a, d) for a in ("gx", "gy", "gz") for d in (1, -1)]
    greeted = []
    for axis, offset in partners:
        greeted.append(beside(axis, offset))
    for d in range(2, span_z - 1):
        greeted.append(beside("gz", d))
    for d in range(2, span_y - 1):
        greeted.append(beside("gy", d))
    for d in range(2, span_x - 1):
        greeted.append(beside("gx", d))
    with jax.named_scope("entry"):
        for device in greeted:
            pl.semaphore_signal(barrier, 1, device_id=device)
        pl.semaphore_wait(barrier, len(greeted))

    lane = lax.broadcasted_iota(jnp.int32, (GROUP, 128), 1)
    low_half = lane < KEYS

    def pack_z(k, g, x, tiles):
        packed = jnp.zeros((GROUP, 128), F32)
        for y in range(size_y):
            moved = pltpu.roll(tiles[y], (8 * y + 4) % 128, 1)
            packed = jnp.where((lane >= 8 * y) & (lane < 8 * y + 8), moved, packed)
        z_pack[k, g, x] = packed.astype(BF16)

    def send_edges(k, g):
        for side in range(2):
            y_copy(k, g, side).start()
            z_copy(k, g, side).start()

    def gather(k, chosen):
        def one(x, acc):
            row = jnp.concatenate(
                [
                    jnp.concatenate([field[k, g, 4 + x, y] for y in range(size_y)], axis=1)
                    for g in chosen
                ],
                axis=0,
            )
            return acc + jnp.dot(row, gather_op[x], preferred_element_type=F32)

        none = jnp.zeros((GROUP * len(chosen), val_ref.shape[1]), F32)
        picked = lax.fori_loop(0, size_x, one, none)
        high, low = split(picked * val_ref[...])
        both = jnp.dot(high, key_in[...], preferred_element_type=F32)
        both = both + jnp.dot(low, key_in[...], preferred_element_type=F32)
        parts = [both[GROUP * i : GROUP * (i + 1)] for i in range(len(chosen))]
        return jnp.concatenate(
            [jnp.where(low_half[:8], part[:8], part[8:]) for part in parts], axis=0
        )

    def first_pump(pieces):
        for i in pieces:
            for side in range(2):
                x_copy(0, i // size_x, i % size_x, side).start()

    for g in range(groups):
        load_copy(g).wait()
        if g < 2:
            first_pump(range(size_x * g, size_x * (g + 1)))

    def first_pack(i, carry):
        g, x = lax.div(i, size_x), lax.rem(i, size_x)
        pack_z(0, g, x, [field[0, g, 4 + x, y].astype(F32) for y in range(size_y)])
        return carry

    with jax.named_scope("first_pack"):
        lax.fori_loop(0, groups * size_x, first_pack, 0)
        for g in range(groups):
            send_edges(0, g)

    atoms = atom_ref[...]
    bits_a, bits_y, bits_z = (n.bit_length() - 1 for n in (A_DEV, span_y, span_z))
    owner = atoms >> bits_a
    key = (
        (((owner >> (bits_y + bits_z)) - here["gx"] + 1) * 3
         + ((owner >> bits_z) & (span_y - 1)) - here["gy"] + 1) * 3
        + (owner & (span_z - 1)) - here["gz"] + 1
    ) * A_DEV + (atoms & (A_DEV - 1))
    entries = atoms.shape[1]
    key_rows = lax.broadcasted_iota(jnp.int32, (2 * KEYS, entries), 0)
    entry_key = jnp.where((key_rows & (KEYS - 1)) == key, 1.0, 0.0)
    key_out[...] = jnp.where(key_rows < KEYS, entry_key, 0.0).astype(BF16)
    key_in[...] = entry_key.T.astype(BF16)
    cells = cell_ref[...]
    z_rows = lax.broadcasted_iota(jnp.int32, (128, entries), 0)
    cell_rows = jnp.broadcast_to(cells.astype(F32), (128, entries)).T.astype(jnp.int32)
    z_lanes = lax.broadcasted_iota(jnp.int32, (entries, 128), 1)

    def build(r, carry):
        x, y = lax.div(r, size_y), lax.rem(r, size_y)
        hot = jnp.where(z_rows + r * 128 == cells, 1.0, 0.0).astype(BF16)
        gather_op[x, pl.ds(pl.multiple_of(y * 128, 128), 128)] = hot
        hot = jnp.where(z_lanes + r * 128 == cell_rows, 1.0, 0.0).astype(BF16)
        scatter_op[r] = hot
        return carry

    with jax.named_scope("build"):
        lax.fori_loop(0, size_x * size_y, build, 0)

    linear = (here["gx"] * SPAN["gy"] + here["gy"]) * SPAN["gz"] + here["gz"]
    row = coup_ref[pl.ds(lax.div(linear * A_DEV, 128), 1)]
    at = lax.rem(linear * A_DEV, 128)
    row = jnp.broadcast_to(row, (8, 128))
    lane8 = lane[:8]
    for half in range(2):
        shift = lax.rem(OWN_LANE + half * KEYS - at + 128, 128)
        moved = pltpu.roll(row, shift, 1)
        base = OWN_LANE + half * KEYS
        keep = (lane8 >= base) & (lane8 < base + A_DEV)
        part = jnp.where(keep, moved, 0.0) / FILTER_HALF
        coup_row[...] = part if half == 0 else coup_row[...] + part
    potq[...] = (pot_ref[...] - (FILTER_CENTRE + 1.5 * STENCIL[0])) / FILTER_HALF

    def combine(stage, own, from_low, from_high):
        shift = STAGES[stage][1]
        if stage < 3:
            total = own + pltpu.roll(from_low, 128 - shift, 1) + pltpu.roll(from_high, shift, 1)
            if stage == 2:
                scale = coup_row[...]
                total = total * jnp.concatenate([scale] * (own.shape[0] // 8), axis=0)
            return total
        return own + pltpu.roll(from_low, 128 - shift, 1) + pltpu.roll(from_high, shift, 1)

    def write_table(k, g, packed):
        turned = pltpu.roll(packed, KEYS, 1)
        first_bands = jnp.where(low_half[:8], packed, turned)
        other_bands = jnp.where(low_half[:8], turned, packed)
        whole = jnp.concatenate([first_bands, other_bands], axis=0)
        high, low = split(whole)
        back = jnp.dot(high, key_out[...], preferred_element_type=F32)
        back = back + jnp.dot(low, key_out[...], preferred_element_type=F32)
        back = back * val_ref[...]
        high = back.astype(BF16).astype(F32)
        table[k, g] = jnp.concatenate([high, back - high], axis=0).astype(BF16)

    def advance(chain, stage):
        for side in range(2):
            q_copy(chain, stage, side).wait()
        result = combine(
            stage, q_send[chain, stage], q_recv[chain, stage, 0], q_recv[chain, stage, 1]
        )
        if stage < 5:
            q_send[chain, stage + 1] = result
            for side in range(2):
                q_copy(chain, stage + 1, side).start()
        else:
            write_table(1 + lax.div(chain, groups), lax.rem(chain, groups), result)

    with jax.named_scope("first_exchange"):
        q0_send[0] = gather(0, range(groups))
        for stage in range(6):
            for side in range(2):
                q0_copy(stage, side).start()
            if stage == 2:
                first_pump(range(2 * size_x, 2 * size_x + 2))
            if stage == 3:
                first_pump(range(2 * size_x + 2, groups * size_x))
            for side in range(2):
                q0_copy(stage, side).wait()
            result = combine(stage, q0_send[stage], q0_recv[stage, 0], q0_recv[stage, 1])
            if stage < 5:
                q0_send[stage + 1] = result
            else:
                for g in range(groups):
                    write_table(0, g, result[8 * g : 8 * g + 8])

    stencil = [-0.5 * c / FILTER_HALF for c in STENCIL]

    def one_x(k, g, x):
        back = jnp.maximum(k - 1, 0)
        own = [field[k, g, 4 + x, y] for y in range(size_y)]
        ownf = [v.astype(F32) for v in own]
        low_y = [y_halo[k, g, 0, x, i].astype(F32) for i in range(4)]
        high_y = [y_halo[k, g, 1, x, i].astype(F32) for i in range(4)]
        line = low_y + ownf + high_y
        from_low = z_halo[k, g, 0, x].astype(F32) * first["gz"]
        from_high = z_halo[k, g, 1, x].astype(F32) * last["gz"]
        halo = jnp.where((lane & 7) < 4, from_low, from_high)
        turned = [halo if y == 0 else pltpu.roll(halo, 128 - 8 * y, 1) for y in range(size_y)]
        left = jnp.concatenate(
            [jnp.concatenate([own[y], turned[y].astype(BF16)], axis=1) for y in range(size_y)],
            axis=0,
        )
        z_term = jnp.dot(left, wz_ref[...], preferred_element_type=F32)
        scale = jnp.where(k == 0, 1.0, 2.0).astype(F32)
        keep = jnp.where(k == 0, 0.0, 1.0).astype(F32)
        c_low, c_high = [], []
        for m in range(1, 5):
            c_low.append(jnp.where(x - m >= 0, 1.0, first["gx"]) * stencil[m])
            c_high.append(jnp.where(x + m <= 3, 1.0, last["gx"]) * stencil[m])
        tiles = []
        coef = table[k, g]
        for y in range(size_y):
            total = ownf[y] * potq[x, pl.ds(y, 1)]
            for m in range(1, 5):
                total += c_low[m - 1] * field[k, g, 4 + x - m, y].astype(F32)
                total += c_high[m - 1] * field[k, g, 4 + x + m, y].astype(F32)
                under, over = line[4 + y - m], line[4 + y + m]
                if y - m < 0:
                    under = under * first["gy"]
                if y + m > size_y - 1:
                    over = over * last["gy"]
                total += stencil[m] * (under + over)
            z_part = z_term[GROUP * y : GROUP * (y + 1)]
            total += z_part[:, :128] + z_part[:, 128:]
            back_part = jnp.dot(
                coef, scatter_op[x * size_y + y], preferred_element_type=F32
            )
            total += back_part[:GROUP] + back_part[GROUP:]
            before = field[back, g, 4 + x, y].astype(F32)
            tile = (scale * total - keep * before).astype(BF16)
            field[k + 1, g, 4 + x, y] = tile
            tiles.append(tile)

        @pl.when(k < DEGREE - 1)
        def _():
            pack_z(k + 1, g, x, [field[k + 1, g, 4 + x, y].astype(F32) for y in range(size_y)])

    def slot(s, carry):
        k, g = lax.div(s, groups), lax.rem(s, groups)
        for side in range(2):
            for x in range(size_x):
                x_copy(k, g, x, side).wait_recv()
            y_copy(k, g, side).wait()
            z_copy(k, g, side).wait()

        def batch(stages):
            for age, stage in zip((3, 2, 1), stages):
                chain = s - age

                @pl.when((chain >= 0) & (chain < (DEGREE - 1) * groups))
                def _(chain=chain, stage=stage):
                    advance(chain, stage)

        def x_step(x, c):
            one_x(k, g, x)
            return c

        def pump(done, pieces):
            @pl.when((done >= 0) & (done < (DEGREE - 1) * groups))
            def _():
                for x in pieces:
                    for side in range(2):
                        x_copy(lax.div(done, groups) + 1, lax.rem(done, groups), x, side).start()

        lax.fori_loop(0, size_x // 2, x_step, 0)
        batch((4, 2, 0))
        pump(s - 1, (2, 3))
        lax.fori_loop(size_x // 2, size_x, x_step, 0)

        @pl.when(k < DEGREE - 1)
        def _():
            send_edges(k + 1, g)
            q_send[s, 0] = gather(k + 1, (g,))
            for side in range(2):
                q_copy(s, 0, side).start()

        batch((5, 3, 1))
        pump(s, (0, 1))
        return carry

    lax.fori_loop(0, DEGREE * groups, slot, 0)
    for g in range(groups):
        out_copy(g).start()

    def gram_part(x, acc):
        rows = jnp.concatenate(
            [
                jnp.concatenate([field[DEGREE, g, 4 + x, y] for y in range(size_y)], axis=1)
                for g in range(groups)
            ],
            axis=0,
        )
        nt = (((1,), (1,)), ((), ()))
        return acc + lax.dot_general(rows, rows, nt, preferred_element_type=F32)

    bands = groups * GROUP
    with jax.named_scope("gram_local"):
        gram = lax.fori_loop(0, size_x, gram_part, jnp.zeros((bands, bands), F32))
        gram = gram * (1.0 / float(size_x * size_y * 128 * span_x * span_y * span_z))
    packed = jnp.concatenate([gram[: bands // 2], gram[bands // 2 :]], axis=1)
    piece = bands // 2 // (span_y * span_z)
    for i in range(span_y * span_z):
        g_part[i // span_y, i % span_y] = packed[i * piece : (i + 1) * piece]

    def exchange(count, me, outgoing, landing, sends, recvs, place):
        def copy(other):
            return pltpu.make_async_remote_copy(
                outgoing(other), landing.at[me], sends.at[other], recvs.at[me], device_id=place(other)
            )

        def arrival(other):
            return pltpu.make_async_remote_copy(
                outgoing(other), landing.at[other], sends.at[other], recvs.at[other],
                device_id=place(other),
            )

        others = [lax.rem(me + d, count) for d in range(1, count)]
        for other in others:
            copy(other).start()
        return others, copy, arrival

    def summed(landing, count):
        total = landing[0]
        for i in range(1, count):
            total = total + landing[i]
        return total

    def finish(parts):
        others, copy, arrival = parts
        for other in others:
            arrival(other).wait_recv()
        for other in others:
            copy(other).wait_send()

    with jax.named_scope("gram_sum"):
        at_z, at_y, at_x = here["gz"], here["gy"], here["gx"]
        run = exchange(span_z, at_z, lambda o: g_part.at[o], r_z, sz.at[0], rz.at[0], lambda o: {"gz": o})
        r_z[at_z] = g_part[at_z]
        finish(run)
        s_z[...] = summed(r_z, span_z)
        run = exchange(span_y, at_y, lambda o: s_z.at[o], r_y, sy.at[0], ry.at[0], lambda o: {"gy": o})
        r_y[at_y] = s_z[at_y]
        finish(run)
        s_y[...] = summed(r_y, span_y)
        run = exchange(span_x, at_x, lambda o: s_y, r_x, sx, rx, lambda o: {"gx": o})
        r_x[at_x] = s_y[...]
        finish(run)
        g_all[at_z, at_y] = summed(r_x, span_x)
        run = exchange(span_y, at_y, lambda o: g_all.at[at_z, at_y], g_all.at[at_z], sy.at[1], ry.at[1], lambda o: {"gy": o})
        finish(run)
        run = exchange(span_z, at_z, lambda o: g_all.at[at_z], g_all, sz.at[1], rz.at[1], lambda o: {"gz": o})
        finish(run)
        for i in range(span_y * span_z):
            line = g_all[i // span_y, i % span_y]
            gram_ref[pl.ds(i * piece, piece), :] = line[:, :bands]
            gram_ref[pl.ds(bands // 2 + i * piece, piece), :] = pltpu.roll(line, bands, 1)[:, :bands]

    def close(i, c):
        k, g = lax.div(i, groups), lax.rem(i, groups)
        for side in range(2):
            for x in range(size_x):
                x_copy(k, g, x, side).wait_send()
        return c

    with jax.named_scope("close"):
        lax.fori_loop(0, DEGREE * groups, close, 0)
        for g in range(groups):
            out_copy(g).wait()


def z_weights(size_z):
    coef = [-0.5 * c / FILTER_HALF for c in STENCIL]
    whole = np.zeros((2 * size_z, size_z), np.float32)
    for z in range(size_z):
        for m in range(1, 5):
            for source in (z - m, z + m):
                if source < 0:
                    at = size_z + 4 + source
                elif source >= size_z:
                    at = size_z + 4 + source - size_z
                else:
                    at = source
                whole[at, z] = coef[m]
    high = whole.astype(ml_dtypes.bfloat16)
    low = (whole - high.astype(np.float32)).astype(ml_dtypes.bfloat16)
    return np.concatenate([high, low], axis=1)


def shards(bands, potential, coupling, proj_atom, proj_cell, proj_value):
    count, size_x, size_y, size_z = bands.shape
    entries = proj_atom.shape[1]
    groups = count // GROUP
    chains = (DEGREE - 1) * groups
    grouped = bands.reshape(groups, GROUP, size_x, size_y, size_z).transpose(0, 2, 3, 1, 4)
    vmem = pl.BlockSpec(memory_space=pltpu.VMEM)
    anywhere = pl.BlockSpec(memory_space=pl.ANY)
    dma = pltpu.SemaphoreType.DMA
    span_x, span_y, span_z = SPAN["gx"], SPAN["gy"], SPAN["gz"]
    rows = 8 * groups
    piece = count // 2 // (span_y * span_z)
    out, gram = pl.pallas_call(
        kernel,
        out_shape=(
            jax.ShapeDtypeStruct(grouped.shape, BF16),
            jax.ShapeDtypeStruct((count, count), F32),
        ),
        in_specs=[anywhere] + [vmem] * 6,
        out_specs=(anywhere, vmem),
        scratch_shapes=[
            pltpu.VMEM((DEGREE + 1, groups, 12, size_y, GROUP, size_z), BF16),
            pltpu.VMEM((DEGREE, groups, 2, size_x, 4, GROUP, size_z), BF16),
            pltpu.VMEM((DEGREE, groups, size_x, GROUP, size_z), BF16),
            pltpu.VMEM((DEGREE, groups, 2, size_x, GROUP, size_z), BF16),
            pltpu.VMEM((size_x, size_y * size_z, entries), BF16),
            pltpu.VMEM((size_x * size_y, entries, size_z), BF16),
            pltpu.VMEM((entries, 2 * KEYS), BF16),
            pltpu.VMEM((2 * KEYS, entries), BF16),
            pltpu.VMEM((DEGREE, groups, 2 * GROUP, entries), BF16),
            pltpu.VMEM((8, 128), F32),
            pltpu.VMEM((size_x, size_y, size_z), F32),
            pltpu.VMEM((chains, 6, 8, 128), F32),
            pltpu.VMEM((chains, 6, 2, 8, 128), F32),
            pltpu.VMEM((6, rows, 128), F32),
            pltpu.VMEM((6, 2, rows, 128), F32),
            pltpu.VMEM((span_z, span_y, piece, 128), F32),
            pltpu.VMEM((span_z, span_y, piece, 128), F32),
            pltpu.VMEM((span_y, piece, 128), F32),
            pltpu.VMEM((span_y, piece, 128), F32),
            pltpu.VMEM((piece, 128), F32),
            pltpu.VMEM((span_x, piece, 128), F32),
            pltpu.VMEM((span_z, span_y, piece, 128), F32),
            dma((groups,)),
            dma((groups,)),
            dma((DEGREE, groups, size_x, 2)),
            dma((DEGREE, groups, size_x, 2)),
            dma((DEGREE, groups, 2)),
            dma((DEGREE, groups, 2)),
            dma((DEGREE, groups, 2)),
            dma((DEGREE, groups, 2)),
            dma((chains, 6, 2)),
            dma((chains, 6, 2)),
            dma((6, 2)),
            dma((6, 2)),
            dma((2, span_z)),
            dma((2, span_z)),
            dma((2, span_y)),
            dma((2, span_y)),
            dma((span_x,)),
            dma((span_x,)),
        ],
        compiler_params=pltpu.CompilerParams(
            collective_id=0, has_side_effects=True, vmem_limit_bytes=48 * 1024 * 1024
        ),
    )(
        grouped,
        potential,
        coupling.reshape(-1, 128),
        proj_atom,
        proj_cell,
        proj_value,
        jnp.asarray(z_weights(size_z)),
    )
    filtered = out.transpose(0, 3, 1, 2, 4).reshape(bands.shape)
    return filtered, gram


def solution(mesh):
    SPAN.update(mesh.shape)
    in_specs = (
        P(None, "gx", "gy", "gz"),
        P("gx", "gy", "gz"),
        P(),
        P(("gx", "gy", "gz"), None),
        P(("gx", "gy", "gz"), None),
        P(("gx", "gy", "gz"), None),
    )
    out_specs = (P(None, "gx", "gy", "gz"), P())
    return jax.shard_map(shards, mesh=mesh, in_specs=in_specs, out_specs=out_specs, check_vma=False)
```

```python
import jax
import jax.numpy as jnp
import ml_dtypes
import numpy as np
from jax import lax
from jax.experimental import pallas as pl
from jax.experimental.pallas import tpu as pltpu
from jax.sharding import PartitionSpec as P

A_DEV = 2
DEGREE = 3
STENCIL = (-205.0 / 72.0, 8.0 / 5.0, -1.0 / 5.0, 8.0 / 315.0, -1.0 / 560.0)
FILTER_CENTRE = 8.25
FILTER_HALF = 7.75

GROUP = 16
KEYS = 64
SPAN = {}
PLANE = [(dy, dz) for dy in (-1, 0, 1) for dz in (-1, 0, 1) if dy or dz]
ACROSS = [({"gy": dy, "gz": dz}, 6 * dy + 2 * dz) for dy, dz in PLANE]
ALONG = [({"gx": 1}, 18), ({"gx": -1}, -18)]
STAGES = (ACROSS, ALONG, ALONG, ACROSS)
OWN_LANE = 26
F32 = jnp.float32
BF16 = jnp.bfloat16


def beside(offsets):
    return {
        axis: lax.rem(lax.axis_index(axis) + d + SPAN[axis], SPAN[axis])
        for axis, d in offsets.items()
    }


def split(value):
    high = value.astype(BF16)
    return high, (value - high.astype(F32)).astype(BF16)


def kernel(
    y0_ref, pot_ref, coup_ref, atom_ref, cell_ref, val_ref, wz_ref,
    out_ref, gram_ref,
    field, y_halo, z_pack, z_halo, gather_op, scatter_op, key_in, key_out, table, coup_all, coup_row, potq,
    q_send, q_recv, q0_send, q0_recv,
    g_part, r_z, s_z, r_y, s_y, r_x, g_all,
    load_sem, out_sem, x_ss, x_rs, y_ss, y_rs, z_ss, z_rs, q_ss, q_rs, q0_ss, q0_rs,
    sz, rz, sy, ry, sx, rx, token,
):
    groups, size_x, size_y = field.shape[1], 4, field.shape[3]
    span_x, span_y, span_z = SPAN["gx"], SPAN["gy"], SPAN["gz"]
    here = {axis: lax.axis_index(axis) for axis in SPAN}
    first = {a: jnp.where(here[a] == 0, 0.0, 1.0).astype(F32) for a in SPAN}
    last = {a: jnp.where(here[a] == SPAN[a] - 1, 0.0, 1.0).astype(F32) for a in SPAN}

    def load_copy(g):
        return pltpu.make_async_copy(y0_ref.at[g], field.at[0, g, pl.ds(4, 4)], load_sem.at[g])

    def out_copy(g):
        return pltpu.make_async_copy(
            field.at[DEGREE, g, pl.ds(4, 4)], out_ref.at[g], out_sem.at[g]
        )

    def x_copy(k, g, half, side):
        return pltpu.make_async_remote_copy(
            field.at[k, g, pl.ds(4 + 2 * half, 2)],
            field.at[k, g, pl.ds(2 * half + 8 * side, 2)],
            x_ss.at[k, g, half, side],
            x_rs.at[k, g, half, side],
            device_id=beside({"gx": 1 - 2 * side}),
        )

    def y_copy(k, g, side):
        rows = pl.ds(12, 4) if side == 0 else pl.ds(0, 4)
        return pltpu.make_async_remote_copy(
            field.at[k, g, pl.ds(4, 4), rows],
            y_halo.at[k, g, side],
            y_ss.at[k, g, side],
            y_rs.at[k, g, side],
            device_id=beside({"gy": 1 - 2 * side}),
        )

    def z_copy(k, g, side):
        return pltpu.make_async_remote_copy(
            z_pack.at[k, g],
            z_halo.at[k, g, side],
            z_ss.at[k, g, side],
            z_rs.at[k, g, side],
            device_id=beside({"gz": 1 - 2 * side}),
        )

    def q_copies(chain, stage):
        return [
            pltpu.make_async_remote_copy(
                q_send.at[chain, stage],
                q_recv.at[chain, stage, i],
                q_ss.at[chain, stage, i],
                q_rs.at[chain, stage, i],
                device_id=beside(offsets),
            )
            for i, (offsets, _) in enumerate(STAGES[stage])
        ]

    def q0_copies(stage):
        return [
            pltpu.make_async_remote_copy(
                q0_send.at[stage],
                q0_recv.at[stage, i],
                q0_ss.at[stage, i],
                q0_rs.at[stage, i],
                device_id=beside(offsets),
            )
            for i, (offsets, _) in enumerate(STAGES[stage])
        ]

    def start(copies):
        for copy in copies:
            copy.start()

    def token_send():
        for side in range(2):
            pl.semaphore_signal(token.at[side], 1, device_id=beside({"gx": 1 - 2 * side}))

    def token_wait():
        for side in range(2):
            pl.semaphore_wait(token.at[side], 1)

    for g in range(groups):
        load_copy(g).start()
    coup_copy = pltpu.make_async_copy(coup_ref, coup_all, load_sem.at[groups])
    coup_copy.start()
    barrier = pltpu.get_barrier_semaphore()
    greeted = [beside(offsets) for offsets, _ in ALONG + ACROSS]
    for device in greeted:
        pl.semaphore_signal(barrier, 1, device_id=device)

    lane = lax.broadcasted_iota(jnp.int32, (GROUP, 128), 1)
    low_half = lane < KEYS

    def pack_z(k, g, x, tiles):
        packed = jnp.zeros((GROUP, 128), F32)
        for y in range(size_y):
            moved = pltpu.roll(tiles[y], (8 * y + 4) % 128, 1)
            packed = jnp.where((lane >= 8 * y) & (lane < 8 * y + 8), moved, packed)
        z_pack[k, g, x] = packed.astype(BF16)

    def send_edges(k, g):
        for side in range(2):
            y_copy(k, g, side).start()
            z_copy(k, g, side).start()

    def gather(k, chosen):
        def one(x, acc):
            row = jnp.concatenate(
                [
                    jnp.concatenate([field[k, g, 4 + x, y] for y in range(size_y)], axis=1)
                    for g in chosen
                ],
                axis=0,
            )
            return acc + jnp.dot(row, gather_op[x], preferred_element_type=F32)

        none = jnp.zeros((GROUP * len(chosen), val_ref.shape[1]), F32)
        picked = lax.fori_loop(0, size_x, one, none, unroll=size_x)
        high, low = split(picked * val_ref[...])
        both = jnp.dot(high, key_in[...], preferred_element_type=F32)
        both = both + jnp.dot(low, key_in[...], preferred_element_type=F32)
        parts = [both[GROUP * i : GROUP * (i + 1)] for i in range(len(chosen))]
        return jnp.concatenate(
            [jnp.where(low_half[:8], part[:8], part[8:]) for part in parts], axis=0
        )

    def pump(k, pieces):
        for i in pieces:
            for side in range(2):
                x_copy(k, i // 2, i % 2, side).start()

    def first_pack(i, carry):
        g, x = lax.div(i, size_x), lax.rem(i, size_x)
        pack_z(0, g, x, [field[0, g, 4 + x, y].astype(F32) for y in range(size_y)])
        return carry

    atoms = atom_ref[...]
    bits_a, bits_y, bits_z = (n.bit_length() - 1 for n in (A_DEV, span_y, span_z))
    owner = atoms >> bits_a
    key = (
        (((owner >> (bits_y + bits_z)) - here["gx"] + 1) * 3
         + ((owner >> bits_z) & (span_y - 1)) - here["gy"] + 1) * 3
        + (owner & (span_z - 1)) - here["gz"] + 1
    ) * A_DEV + (atoms & (A_DEV - 1))
    entries = atoms.shape[1]
    key_rows = lax.broadcasted_iota(jnp.int32, (2 * KEYS, entries), 0)
    entry_key = jnp.where((key_rows & (KEYS - 1)) == key, 1.0, 0.0)
    key_out[...] = jnp.where(key_rows < KEYS, entry_key, 0.0).astype(BF16)
    key_in[...] = entry_key.T.astype(BF16)
    cells = cell_ref[...]
    z_rows = lax.broadcasted_iota(jnp.int32, (128, entries), 0)
    cell_rows = jnp.broadcast_to(cells.astype(F32), (128, entries)).T.astype(jnp.int32)
    z_lanes = lax.broadcasted_iota(jnp.int32, (entries, 128), 1)

    def build(r, carry):
        x, y = lax.div(r, size_y), lax.rem(r, size_y)
        hot = jnp.where(z_rows + r * 128 == cells, 1.0, 0.0).astype(BF16)
        gather_op[x, pl.ds(pl.multiple_of(y * 128, 128), 128)] = hot
        hot = jnp.where(z_lanes + r * 128 == cell_rows, 1.0, 0.0).astype(BF16)
        scatter_op[lax.div(r, 2), :, pl.ds(pl.multiple_of(lax.rem(r, 2) * 128, 128), 128)] = hot
        return carry

    linear = (here["gx"] * SPAN["gy"] + here["gy"]) * SPAN["gz"] + here["gz"]
    coup_copy.wait()
    row = coup_all[pl.ds(lax.div(linear * A_DEV, 128), 1)]
    at = lax.rem(linear * A_DEV, 128)
    row = jnp.broadcast_to(row, (8, 128))
    lane8 = lane[:8]
    for half in range(2):
        shift = lax.rem(OWN_LANE + half * KEYS - at + 128, 128)
        moved = pltpu.roll(row, shift, 1)
        base = OWN_LANE + half * KEYS
        keep = (lane8 >= base) & (lane8 < base + A_DEV)
        part = jnp.where(keep, moved, 0.0) / FILTER_HALF
        coup_row[...] = part if half == 0 else coup_row[...] + part
    potq[...] = (pot_ref[...] - (FILTER_CENTRE + 1.5 * STENCIL[0])) / FILTER_HALF

    pl.semaphore_wait(barrier, len(greeted))
    token_send()

    def pump(k, pieces):
        for i in pieces:
            for side in range(2):
                x_copy(k, i // 2, i % 2, side).start()

    for g in range(groups):
        load_copy(g).wait()
        if g == 0:
            pump(0, (0, 1))

    with jax.named_scope("build"):
        lax.fori_loop(0, size_x * size_y, build, 0)

    def combine(stage, own, arrived):
        total = own
        for (_, shift), part in zip(STAGES[stage], arrived):
            total = total + pltpu.roll(part, (128 - shift) % 128, 1)
        if stage == 1:
            total = total * jnp.concatenate([coup_row[...]] * (own.shape[0] // 8), axis=0)
        return total

    def write_table(k, g, packed):
        turned = pltpu.roll(packed, KEYS, 1)
        first_bands = jnp.where(low_half[:8], packed, turned)
        other_bands = jnp.where(low_half[:8], turned, packed)
        whole = jnp.concatenate([first_bands, other_bands], axis=0)
        high, low = split(whole)
        back = jnp.dot(high, key_out[...], preferred_element_type=F32)
        back = back + jnp.dot(low, key_out[...], preferred_element_type=F32)
        back = back * val_ref[...]
        high = back.astype(BF16).astype(F32)
        table[k, g] = jnp.concatenate([high, back - high], axis=0).astype(BF16)

    def advance(chain, stage):
        for copy in q_copies(chain, stage):
            copy.wait_recv()
        arrived = [q_recv[chain, stage, i] for i in range(len(STAGES[stage]))]
        result = combine(stage, q_send[chain, stage], arrived)
        if stage < 3:
            q_send[chain, stage + 1] = result
            start(q_copies(chain, stage + 1))
        else:
            k, half = 1 + lax.div(chain, 2), lax.rem(chain, 2)
            for i in range(2):
                write_table(k, 2 * half + i, result[8 * i : 8 * i + 8])

    with jax.named_scope("first_exchange"):
        q0_send[0] = gather(0, range(groups))
        for stage in range(4):
            start(q0_copies(stage))
            if stage == 0:
                pump(0, (2,))
                lax.fori_loop(0, groups * size_x, first_pack, 0, unroll=2)
                for g in range(groups):
                    send_edges(0, g)
            if stage == 1:
                pump(0, (3,))
            if stage == 2:
                pump(0, range(4, 8))
            token_wait()
            token_send()
            for copy in q0_copies(stage):
                copy.wait_recv()
            arrived = [q0_recv[stage, i] for i in range(len(STAGES[stage]))]
            result = combine(stage, q0_send[stage], arrived)
            if stage < 3:
                q0_send[stage + 1] = result
            else:
                for g in range(groups):
                    write_table(0, g, result[8 * g : 8 * g + 8])

    stencil = [-0.5 * c / FILTER_HALF for c in STENCIL]

    def one_x(k, g, x):
        back = jnp.maximum(k - 1, 0)
        own = [field[k, g, 4 + x, y] for y in range(size_y)]
        ownf = [v.astype(F32) for v in own]
        low_y = [y_halo[k, g, 0, x, i].astype(F32) for i in range(4)]
        high_y = [y_halo[k, g, 1, x, i].astype(F32) for i in range(4)]
        line = low_y + ownf + high_y
        from_low = z_halo[k, g, 0, x].astype(F32) * first["gz"]
        from_high = z_halo[k, g, 1, x].astype(F32) * last["gz"]
        halo = jnp.where((lane & 7) < 4, from_low, from_high)
        turned = [halo if y == 0 else pltpu.roll(halo, 128 - 8 * y, 1) for y in range(size_y)]
        left = jnp.concatenate(
            [jnp.concatenate([own[y], turned[y].astype(BF16)], axis=1) for y in range(size_y)],
            axis=0,
        )
        z_term = jnp.dot(left, wz_ref[...], preferred_element_type=F32)
        scale = jnp.where(k == 0, 1.0, 2.0).astype(F32)
        keep = jnp.where(k == 0, 0.0, 1.0).astype(F32)
        c_low, c_high = [], []
        for m in range(1, 5):
            c_low.append(jnp.where(x - m >= 0, 1.0, first["gx"]) * stencil[m])
            c_high.append(jnp.where(x + m <= 3, 1.0, last["gx"]) * stencil[m])
        tiles = []
        coef = table[k, g]
        for pair in range(size_y // 2):
            back_part = jnp.dot(
                coef, scatter_op[x * (size_y // 2) + pair], preferred_element_type=F32
            )
            for i in range(2):
                y = 2 * pair + i
                total = ownf[y] * potq[x, pl.ds(y, 1)]
                for m in range(1, 5):
                    total += c_low[m - 1] * field[k, g, 4 + x - m, y].astype(F32)
                    total += c_high[m - 1] * field[k, g, 4 + x + m, y].astype(F32)
                    under, over = line[4 + y - m], line[4 + y + m]
                    if y - m < 0:
                        under = under * first["gy"]
                    if y + m > size_y - 1:
                        over = over * last["gy"]
                    total += stencil[m] * (under + over)
                z_part = z_term[GROUP * y : GROUP * (y + 1)]
                total += z_part[:, :128] + z_part[:, 128:]
                mine = back_part[:, 128 * i : 128 * (i + 1)]
                total += mine[:GROUP] + mine[GROUP:]
                before = field[back, g, 4 + x, y].astype(F32)
                tiles.append((scale * total - keep * before).astype(BF16))
        for y in range(size_y):
            field[k + 1, g, 4 + x, y] = tiles[y]
        pack_z(k + 1, g, x, [tile.astype(F32) for tile in tiles])

    def finish_group(k, g):
        for side in range(2):
            for half in range(2):
                x_copy(k, g, half, side).wait_recv()
            y_copy(k, g, side).wait()
            z_copy(k, g, side).wait()

        def x_step(x, c):
            one_x(k, g, x)
            return c

        lax.fori_loop(0, size_x, x_step, 0, unroll=size_x)

    def round_of(k, carry):
        more = k < DEGREE - 1

        def begin(half):
            chain = 2 * k + half
            q_send[chain, 0] = gather(k + 1, (2 * half, 2 * half + 1))
            start(q_copies(chain, 0))

        @pl.when(k > 0)
        def _():
            advance(2 * k - 1, 1)
            pump(k, (7,))

        token_wait()
        token_send()
        finish_group(k, 0)

        @pl.when(more)
        def _():
            pump(k + 1, (0, 1))
            send_edges(k + 1, 0)

        @pl.when(k > 0)
        def _():
            advance(2 * k - 1, 2)

        token_wait()
        token_send()
        finish_group(k, 1)

        @pl.when(more)
        def _():
            begin(0)
            pump(k + 1, (2,))
            send_edges(k + 1, 1)

        @pl.when(k > 0)
        def _():
            advance(2 * k - 1, 3)

        finish_group(k, 2)

        @pl.when(more)
        def _():
            advance(2 * k, 0)
            pump(k + 1, (3,))
            send_edges(k + 1, 2)

        token_wait()
        token_send()
        finish_group(k, 3)

        @pl.when(more)
        def _():
            advance(2 * k, 1)
            pump(k + 1, (4,))
            send_edges(k + 1, 3)
            begin(1)
            token_wait()
            token_send()
            advance(2 * k, 2)
            advance(2 * k + 1, 0)
            pump(k + 1, (5, 6))
            advance(2 * k, 3)

        return carry

    lax.fori_loop(0, DEGREE, round_of, 0)
    for g in range(groups):
        out_copy(g).start()

    def gram_part(x, acc):
        rows = jnp.concatenate(
            [
                jnp.concatenate([field[DEGREE, g, 4 + x, y] for y in range(size_y)], axis=1)
                for g in range(groups)
            ],
            axis=0,
        )
        nt = (((1,), (1,)), ((), ()))
        return acc + lax.dot_general(rows, rows, nt, preferred_element_type=F32)

    bands = groups * GROUP
    with jax.named_scope("gram_local"):
        gram = lax.fori_loop(0, size_x, gram_part, jnp.zeros((bands, bands), F32), unroll=size_x)
        gram = gram * (1.0 / float(size_x * size_y * 128 * span_x * span_y * span_z))
    packed = jnp.concatenate([gram[: bands // 2], gram[bands // 2 :]], axis=1)
    piece = bands // 2 // (span_y * span_z)
    for i in range(span_y * span_z):
        g_part[i // span_y, i % span_y] = packed[i * piece : (i + 1) * piece]

    def exchange(count, me, outgoing, landing, sends, recvs, place):
        def copy(other):
            return pltpu.make_async_remote_copy(
                outgoing(other), landing.at[me], sends.at[other], recvs.at[me], device_id=place(other)
            )

        def arrival(other):
            return pltpu.make_async_remote_copy(
                outgoing(other), landing.at[other], sends.at[other], recvs.at[other],
                device_id=place(other),
            )

        far_first = sorted(range(1, count), key=lambda d: -min(d, count - d))
        others = [lax.rem(me + d, count) for d in far_first]
        for other in others:
            copy(other).start()
        return others, copy, arrival

    def summed(landing, count):
        total = landing[0]
        for i in range(1, count):
            total = total + landing[i]
        return total

    open_sends = []

    def finish(parts):
        others, copy, arrival = parts
        for other in reversed(others):
            arrival(other).wait_recv()
        open_sends.append((others, copy))

    token_wait()
    with jax.named_scope("gram_sum"):
        at_z, at_y, at_x = here["gz"], here["gy"], here["gx"]
        run = exchange(span_z, at_z, lambda o: g_part.at[o], r_z, sz.at[0], rz.at[0], lambda o: {"gz": o})
        r_z[at_z] = g_part[at_z]
        finish(run)
        s_z[...] = summed(r_z, span_z)
        run = exchange(span_y, at_y, lambda o: s_z.at[o], r_y, sy.at[0], ry.at[0], lambda o: {"gy": o})
        r_y[at_y] = s_z[at_y]
        finish(run)
        s_y[...] = summed(r_y, span_y)
        run = exchange(span_x, at_x, lambda o: s_y, r_x, sx, rx, lambda o: {"gx": o})
        r_x[at_x] = s_y[...]
        finish(run)
        g_all[at_z, at_y] = summed(r_x, span_x)
        run = exchange(span_y, at_y, lambda o: g_all.at[at_z, at_y], g_all.at[at_z], sy.at[1], ry.at[1], lambda o: {"gy": o})
        finish(run)
        run = exchange(span_z, at_z, lambda o: g_all.at[at_z], g_all, sz.at[1], rz.at[1], lambda o: {"gz": o})
        finish(run)
        for i in range(span_y * span_z):
            line = g_all[i // span_y, i % span_y]
            gram_ref[pl.ds(i * piece, piece), :] = line[:, :bands]
            gram_ref[pl.ds(bands // 2 + i * piece, piece), :] = pltpu.roll(line, bands, 1)[:, :bands]

    def close(i, c):
        k, g = lax.div(i, groups), lax.rem(i, groups)
        for side in range(2):
            for half in range(2):
                x_copy(k, g, half, side).wait_send()
        return c

    def close_chain(chain, c):
        for stage in range(4):
            for copy in q_copies(chain, stage):
                copy.wait_send()
        return c

    with jax.named_scope("close"):
        lax.fori_loop(0, DEGREE * groups, close, 0)
        lax.fori_loop(0, 2 * (DEGREE - 1), close_chain, 0)
        for stage in range(4):
            for copy in q0_copies(stage):
                copy.wait_send()
        for others, copy in open_sends:
            for other in others:
                copy(other).wait_send()
        for g in range(groups):
            out_copy(g).wait()


def z_weights(size_z):
    coef = [-0.5 * c / FILTER_HALF for c in STENCIL]
    whole = np.zeros((2 * size_z, size_z), np.float32)
    for z in range(size_z):
        for m in range(1, 5):
            for source in (z - m, z + m):
                if source < 0:
                    at = size_z + 4 + source
                elif source >= size_z:
                    at = size_z + 4 + source - size_z
                else:
                    at = source
                whole[at, z] = coef[m]
    high = whole.astype(ml_dtypes.bfloat16)
    low = (whole - high.astype(np.float32)).astype(ml_dtypes.bfloat16)
    return np.concatenate([high, low], axis=1)


def shards(bands, potential, coupling, proj_atom, proj_cell, proj_value):
    count, size_x, size_y, size_z = bands.shape
    entries = proj_atom.shape[1]
    groups = count // GROUP
    chains = 2 * (DEGREE - 1)
    grouped = bands.reshape(groups, GROUP, size_x, size_y, size_z).transpose(0, 2, 3, 1, 4)
    vmem = pl.BlockSpec(memory_space=pltpu.VMEM)
    anywhere = pl.BlockSpec(memory_space=pl.ANY)
    dma = pltpu.SemaphoreType.DMA
    span_x, span_y, span_z = SPAN["gx"], SPAN["gy"], SPAN["gz"]
    rows = 8 * groups
    piece = count // 2 // (span_y * span_z)
    out, gram = pl.pallas_call(
        kernel,
        out_shape=(
            jax.ShapeDtypeStruct(grouped.shape, BF16),
            jax.ShapeDtypeStruct((count, count), F32),
        ),
        in_specs=[anywhere, vmem, anywhere] + [vmem] * 4,
        out_specs=(anywhere, vmem),
        scratch_shapes=[
            pltpu.VMEM((DEGREE + 1, groups, 12, size_y, GROUP, size_z), BF16),
            pltpu.VMEM((DEGREE, groups, 2, size_x, 4, GROUP, size_z), BF16),
            pltpu.VMEM((DEGREE + 1, groups, size_x, GROUP, size_z), BF16),
            pltpu.VMEM((DEGREE, groups, 2, size_x, GROUP, size_z), BF16),
            pltpu.VMEM((size_x, size_y * size_z, entries), BF16),
            pltpu.VMEM((size_x * size_y // 2, entries, 2 * size_z), BF16),
            pltpu.VMEM((entries, 2 * KEYS), BF16),
            pltpu.VMEM((2 * KEYS, entries), BF16),
            pltpu.VMEM((DEGREE, groups, 2 * GROUP, entries), BF16),
            pltpu.VMEM((coupling.size // 128, 128), F32),
            pltpu.VMEM((8, 128), F32),
            pltpu.VMEM((size_x, size_y, size_z), F32),
            pltpu.VMEM((chains, 4, rows // 2, 128), F32),
            pltpu.VMEM((chains, 4, 8, rows // 2, 128), F32),
            pltpu.VMEM((4, rows, 128), F32),
            pltpu.VMEM((4, 8, rows, 128), F32),
            pltpu.VMEM((span_z, span_y, piece, 128), F32),
            pltpu.VMEM((span_z, span_y, piece, 128), F32),
            pltpu.VMEM((span_y, piece, 128), F32),
            pltpu.VMEM((span_y, piece, 128), F32),
            pltpu.VMEM((piece, 128), F32),
            pltpu.VMEM((span_x, piece, 128), F32),
            pltpu.VMEM((span_z, span_y, piece, 128), F32),
            dma((groups + 1,)),
            dma((groups,)),
            dma((DEGREE, groups, 2, 2)),
            dma((DEGREE, groups, 2, 2)),
            dma((DEGREE, groups, 2)),
            dma((DEGREE, groups, 2)),
            dma((DEGREE, groups, 2)),
            dma((DEGREE, groups, 2)),
            dma((chains, 4, 8)),
            dma((chains, 4, 8)),
            dma((4, 8)),
            dma((4, 8)),
            dma((2, span_z)),
            dma((2, span_z)),
            dma((2, span_y)),
            dma((2, span_y)),
            dma((span_x,)),
            dma((span_x,)),
            pltpu.SemaphoreType.REGULAR((2,)),
        ],
        compiler_params=pltpu.CompilerParams(
            collective_id=0, has_side_effects=True, vmem_limit_bytes=48 * 1024 * 1024
        ),
    )(
        grouped,
        potential,
        coupling.reshape(-1, 128),
        proj_atom,
        proj_cell,
        proj_value,
        jnp.asarray(z_weights(size_z)),
    )
    filtered = out.transpose(0, 3, 1, 2, 4).reshape(bands.shape)
    return filtered, gram


def solution(mesh):
    SPAN.update(mesh.shape)
    in_specs = (
        P(None, "gx", "gy", "gz"),
        P("gx", "gy", "gz"),
        P(),
        P(("gx", "gy", "gz"), None),
        P(("gx", "gy", "gz"), None),
        P(("gx", "gy", "gz"), None),
    )
    out_specs = (P(None, "gx", "gy", "gz"), P())
    return jax.shard_map(shards, mesh=mesh, in_specs=in_specs, out_specs=out_specs, check_vma=False)
```

```python
import jax
import jax.numpy as jnp
import ml_dtypes
import numpy as np
from jax import lax
from jax.experimental import pallas as pl
from jax.experimental.pallas import tpu as pltpu
from jax.sharding import PartitionSpec as P

A_DEV = 2
DEGREE = 3
STENCIL = (-205.0 / 72.0, 8.0 / 5.0, -1.0 / 5.0, 8.0 / 315.0, -1.0 / 560.0)
FILTER_CENTRE = 8.25
FILTER_HALF = 7.75

GROUP = 16
KEYS = 64
SPAN = {}
PLANE = [(dy, dz) for dy in (-1, 0, 1) for dz in (-1, 0, 1) if dy or dz]
ACROSS = [({"gy": dy, "gz": dz}, 6 * dy + 2 * dz) for dy, dz in PLANE]
ALONG = [({"gx": 1}, 18), ({"gx": -1}, -18)]
STAGES = (ACROSS, ALONG, ALONG, ACROSS)
OWN_LANE = 26
F32 = jnp.float32
BF16 = jnp.bfloat16


def beside(offsets):
    return {
        axis: lax.rem(lax.axis_index(axis) + d + SPAN[axis], SPAN[axis])
        for axis, d in offsets.items()
    }


def split(value):
    high = value.astype(BF16)
    return high, (value - high.astype(F32)).astype(BF16)


def kernel(
    y0_ref, pot_ref, coup_ref, atom_ref, cell_ref, val_ref, wz_ref,
    out_ref, gram_ref,
    field, y_halo, z_pack, z_halo, gather_op, scatter_op, key_in, key_out, table, coup_all, coup_row, potq,
    q_send, q_recv, q0_send, q0_recv,
    g_part, r_z, s_z, r_y, s_y, r_x, g_all,
    load_sem, out_sem, x_ss, x_rs, y_ss, y_rs, z_ss, z_rs, q_ss, q_rs, q0_ss, q0_rs,
    sz, rz, sy, ry, sx, rx, token,
):
    groups, size_x, size_y = field.shape[1], 4, field.shape[3]
    span_x, span_y, span_z = SPAN["gx"], SPAN["gy"], SPAN["gz"]
    here = {axis: lax.axis_index(axis) for axis in SPAN}
    first = {a: jnp.where(here[a] == 0, 0.0, 1.0).astype(F32) for a in SPAN}
    last = {a: jnp.where(here[a] == SPAN[a] - 1, 0.0, 1.0).astype(F32) for a in SPAN}

    def load_copy(g):
        return pltpu.make_async_copy(y0_ref.at[g], field.at[0, g, pl.ds(4, 4)], load_sem.at[g])

    def out_copy(g):
        return pltpu.make_async_copy(
            field.at[DEGREE, g, pl.ds(4, 4)], out_ref.at[g], out_sem.at[g]
        )

    def x_copy(k, g, half, side):
        return pltpu.make_async_remote_copy(
            field.at[k, g, pl.ds(4 + 2 * half, 2)],
            field.at[k, g, pl.ds(2 * half + 8 * side, 2)],
            x_ss.at[k, g, half, side],
            x_rs.at[k, g, half, side],
            device_id=beside({"gx": 1 - 2 * side}),
        )

    def y_copy(k, g, side):
        rows = pl.ds(12, 4) if side == 0 else pl.ds(0, 4)
        return pltpu.make_async_remote_copy(
            field.at[k, g, pl.ds(4, 4), rows],
            y_halo.at[k, g, side],
            y_ss.at[k, g, side],
            y_rs.at[k, g, side],
            device_id=beside({"gy": 1 - 2 * side}),
        )

    def z_copy(k, g, side):
        return pltpu.make_async_remote_copy(
            z_pack.at[k, g],
            z_halo.at[k, g, side],
            z_ss.at[k, g, side],
            z_rs.at[k, g, side],
            device_id=beside({"gz": 1 - 2 * side}),
        )

    def q_copies(chain, stage):
        return [
            pltpu.make_async_remote_copy(
                q_send.at[chain, stage],
                q_recv.at[chain, stage, i],
                q_ss.at[chain, stage, i],
                q_rs.at[chain, stage, i],
                device_id=beside(offsets),
            )
            for i, (offsets, _) in enumerate(STAGES[stage])
        ]

    def q0_copies(stage):
        return [
            pltpu.make_async_remote_copy(
                q0_send.at[stage],
                q0_recv.at[stage, i],
                q0_ss.at[stage, i],
                q0_rs.at[stage, i],
                device_id=beside(offsets),
            )
            for i, (offsets, _) in enumerate(STAGES[stage])
        ]

    def start(copies):
        for copy in copies:
            copy.start()

    def token_send():
        for side in range(2):
            pl.semaphore_signal(token.at[side], 1, device_id=beside({"gx": 1 - 2 * side}))

    def token_wait():
        for side in range(2):
            pl.semaphore_wait(token.at[side], 1)

    for g in range(groups):
        load_copy(g).start()
    coup_copy = pltpu.make_async_copy(coup_ref, coup_all, load_sem.at[groups])
    coup_copy.start()
    barrier = pltpu.get_barrier_semaphore()
    greeted = [beside(offsets) for offsets, _ in ALONG + ACROSS]
    for device in greeted:
        pl.semaphore_signal(barrier, 1, device_id=device)

    lane = lax.broadcasted_iota(jnp.int32, (GROUP, 128), 1)
    low_half = lane < KEYS

    def pack_z(k, g, x, tiles):
        packed = jnp.zeros((GROUP, 128), F32)
        for y in range(size_y):
            moved = pltpu.roll(tiles[y], (8 * y + 4) % 128, 1)
            packed = jnp.where((lane >= 8 * y) & (lane < 8 * y + 8), moved, packed)
        z_pack[k, g, x] = packed.astype(BF16)

    def send_edges(k, g):
        for side in range(2):
            y_copy(k, g, side).start()
            z_copy(k, g, side).start()

    def gather(k, chosen):
        def one(x, acc):
            row = jnp.concatenate(
                [
                    jnp.concatenate([field[k, g, 4 + x, y] for y in range(size_y)], axis=1)
                    for g in chosen
                ],
                axis=0,
            )
            return acc + jnp.dot(row, gather_op[x], preferred_element_type=F32)

        none = jnp.zeros((GROUP * len(chosen), val_ref.shape[1]), F32)
        picked = lax.fori_loop(0, size_x, one, none, unroll=size_x)
        high, low = split(picked * val_ref[...])
        both = jnp.dot(high, key_in[...], preferred_element_type=F32)
        both = both + jnp.dot(low, key_in[...], preferred_element_type=F32)
        parts = [both[GROUP * i : GROUP * (i + 1)] for i in range(len(chosen))]
        return jnp.concatenate(
            [jnp.where(low_half[:8], part[:8], part[8:]) for part in parts], axis=0
        )

    def pump(k, pieces):
        for i in pieces:
            for side in range(2):
                x_copy(k, i // 2, i % 2, side).start()

    def first_pack(i, carry):
        g, x = lax.div(i, size_x), lax.rem(i, size_x)
        pack_z(0, g, x, [field[0, g, 4 + x, y].astype(F32) for y in range(size_y)])
        return carry

    atoms = atom_ref[...]
    bits_a, bits_y, bits_z = (n.bit_length() - 1 for n in (A_DEV, span_y, span_z))
    owner = atoms >> bits_a
    key = (
        (((owner >> (bits_y + bits_z)) - here["gx"] + 1) * 3
         + ((owner >> bits_z) & (span_y - 1)) - here["gy"] + 1) * 3
        + (owner & (span_z - 1)) - here["gz"] + 1
    ) * A_DEV + (atoms & (A_DEV - 1))
    entries = atoms.shape[1]
    key_rows = lax.broadcasted_iota(jnp.int32, (2 * KEYS, entries), 0)
    entry_key = jnp.where((key_rows & (KEYS - 1)) == key, 1.0, 0.0)
    key_out[...] = jnp.where(key_rows < KEYS, entry_key, 0.0).astype(BF16)
    key_in[...] = entry_key.T.astype(BF16)
    cells = cell_ref[...]
    z_rows = lax.broadcasted_iota(jnp.int32, (128, entries), 0)
    cell_rows = jnp.broadcast_to(cells.astype(F32), (128, entries)).T.astype(jnp.int32)
    z_lanes = lax.broadcasted_iota(jnp.int32, (entries, 128), 1)

    def build(r, carry):
        x, y = lax.div(r, size_y), lax.rem(r, size_y)
        hot = jnp.where(z_rows + r * 128 == cells, 1.0, 0.0).astype(BF16)
        gather_op[x, pl.ds(pl.multiple_of(y * 128, 128), 128)] = hot
        hot = jnp.where(z_lanes + r * 128 == cell_rows, 1.0, 0.0).astype(BF16)
        scatter_op[lax.div(r, 2), :, pl.ds(pl.multiple_of(lax.rem(r, 2) * 128, 128), 128)] = hot
        return carry

    linear = (here["gx"] * SPAN["gy"] + here["gy"]) * SPAN["gz"] + here["gz"]
    coup_copy.wait()
    row = coup_all[pl.ds(lax.div(linear * A_DEV, 128), 1)]
    at = lax.rem(linear * A_DEV, 128)
    row = jnp.broadcast_to(row, (8, 128))
    lane8 = lane[:8]
    for half in range(2):
        shift = lax.rem(OWN_LANE + half * KEYS - at + 128, 128)
        moved = pltpu.roll(row, shift, 1)
        base = OWN_LANE + half * KEYS
        keep = (lane8 >= base) & (lane8 < base + A_DEV)
        part = jnp.where(keep, moved, 0.0) / FILTER_HALF
        coup_row[...] = part if half == 0 else coup_row[...] + part
    potq[...] = (pot_ref[...] - (FILTER_CENTRE + 1.5 * STENCIL[0])) / FILTER_HALF

    pl.semaphore_wait(barrier, len(greeted))
    token_send()

    def pump(k, pieces):
        for i in pieces:
            for side in range(2):
                x_copy(k, i // 2, i % 2, side).start()

    for g in range(groups):
        load_copy(g).wait()
        if g == 0:
            pump(0, (0, 1))

    with jax.named_scope("build"):
        lax.fori_loop(0, size_x * size_y, build, 0)

    def combine(stage, own, arrived):
        total = own
        for (_, shift), part in zip(STAGES[stage], arrived):
            total = total + pltpu.roll(part, (128 - shift) % 128, 1)
        if stage == 1:
            total = total * jnp.concatenate([coup_row[...]] * (own.shape[0] // 8), axis=0)
        return total

    def write_table(k, g, packed):
        count = packed.shape[0] // 8
        turned = pltpu.roll(packed, KEYS, 1)
        low = lax.broadcasted_iota(jnp.int32, packed.shape, 1) < KEYS
        first_bands = jnp.where(low, packed, turned)
        other_bands = jnp.where(low, turned, packed)
        whole = jnp.concatenate(
            [
                part[8 * i : 8 * i + 8]
                for i in range(count)
                for part in (first_bands, other_bands)
            ],
            axis=0,
        )
        high, low = split(whole)
        back = jnp.dot(high, key_out[...], preferred_element_type=F32)
        back = back + jnp.dot(low, key_out[...], preferred_element_type=F32)
        back = back * val_ref[...]
        high = back.astype(BF16).astype(F32)
        rest = back - high
        for i in range(count):
            rows = slice(GROUP * i, GROUP * (i + 1))
            table[k, g + i] = jnp.concatenate([high[rows], rest[rows]], axis=0).astype(BF16)

    def advance(chain, stage):
        for copy in q_copies(chain, stage):
            copy.wait_recv()
        arrived = [q_recv[chain, stage, i] for i in range(len(STAGES[stage]))]
        result = combine(stage, q_send[chain, stage], arrived)
        if stage < 3:
            q_send[chain, stage + 1] = result
            start(q_copies(chain, stage + 1))
        else:
            k, half = 1 + lax.div(chain, 2), lax.rem(chain, 2)
            write_table(k, 2 * half, result)

    with jax.named_scope("first_exchange"):
        q0_send[0] = gather(0, range(groups))
        for stage in range(4):
            start(q0_copies(stage))
            if stage == 0:
                pump(0, (2,))
                lax.fori_loop(0, groups * size_x, first_pack, 0, unroll=2)
                for g in range(groups):
                    send_edges(0, g)
            if stage == 1:
                pump(0, (3,))
            if stage == 2:
                pump(0, range(4, 8))
            token_wait()
            token_send()
            for copy in q0_copies(stage):
                copy.wait_recv()
            arrived = [q0_recv[stage, i] for i in range(len(STAGES[stage]))]
            result = combine(stage, q0_send[stage], arrived)
            if stage < 3:
                q0_send[stage + 1] = result
            else:
                write_table(0, 0, result)

    stencil = [-0.5 * c / FILTER_HALF for c in STENCIL]

    def one_x(k, g, x):
        back = jnp.maximum(k - 1, 0)
        own = [field[k, g, 4 + x, y] for y in range(size_y)]
        ownf = [v.astype(F32) for v in own]
        low_y = [y_halo[k, g, 0, x, i].astype(F32) for i in range(4)]
        high_y = [y_halo[k, g, 1, x, i].astype(F32) for i in range(4)]
        line = low_y + ownf + high_y
        from_low = z_halo[k, g, 0, x].astype(F32) * first["gz"]
        from_high = z_halo[k, g, 1, x].astype(F32) * last["gz"]
        halo = jnp.where((lane & 7) < 4, from_low, from_high)
        turned = [halo if y == 0 else pltpu.roll(halo, 128 - 8 * y, 1) for y in range(size_y)]
        left = jnp.concatenate(
            [jnp.concatenate([own[y], turned[y].astype(BF16)], axis=1) for y in range(size_y)],
            axis=0,
        )
        z_term = jnp.dot(left, wz_ref[...], preferred_element_type=F32)
        scale = jnp.where(k == 0, 1.0, 2.0).astype(F32)
        keep = jnp.where(k == 0, 0.0, 1.0).astype(F32)
        c_low, c_high = [], []
        for m in range(1, 5):
            c_low.append(jnp.where(x - m >= 0, 1.0, first["gx"]) * stencil[m])
            c_high.append(jnp.where(x + m <= 3, 1.0, last["gx"]) * stencil[m])
        tiles = []
        coef = table[k, g]
        for pair in range(size_y // 2):
            back_part = jnp.dot(
                coef, scatter_op[x * (size_y // 2) + pair], preferred_element_type=F32
            )
            for i in range(2):
                y = 2 * pair + i
                total = ownf[y] * potq[x, pl.ds(y, 1)]
                for m in range(1, 5):
                    total += c_low[m - 1] * field[k, g, 4 + x - m, y].astype(F32)
                    total += c_high[m - 1] * field[k, g, 4 + x + m, y].astype(F32)
                    under, over = line[4 + y - m], line[4 + y + m]
                    if y - m < 0:
                        under = under * first["gy"]
                    if y + m > size_y - 1:
                        over = over * last["gy"]
                    total += stencil[m] * (under + over)
                z_part = z_term[GROUP * y : GROUP * (y + 1)]
                total += z_part[:, :128] + z_part[:, 128:]
                mine = back_part[:, 128 * i : 128 * (i + 1)]
                total += mine[:GROUP] + mine[GROUP:]
                before = field[back, g, 4 + x, y].astype(F32)
                tiles.append((scale * total - keep * before).astype(BF16))
        for y in range(size_y):
            field[k + 1, g, 4 + x, y] = tiles[y]
        pack_z(k + 1, g, x, [tile.astype(F32) for tile in tiles])

    def finish_group(k, g):
        for side in range(2):
            for half in range(2):
                x_copy(k, g, half, side).wait_recv()
            y_copy(k, g, side).wait()
            z_copy(k, g, side).wait()

        def x_step(x, c):
            one_x(k, g, x)
            return c

        lax.fori_loop(0, size_x, x_step, 0, unroll=size_x)

    def round_of(k, carry):
        more = k < DEGREE - 1

        def begin(half):
            chain = 2 * k + half
            q_send[chain, 0] = gather(k + 1, (2 * half, 2 * half + 1))
            start(q_copies(chain, 0))

        def pump_first(pieces):
            @pl.when(k == 0)
            def _():
                pump(k + 1, pieces)

        def pump_later(pieces):
            @pl.when(k > 0)
            def _():
                pump(k + 1, pieces)

        @pl.when(k > 0)
        def _():
            advance(2 * k - 1, 1)

            @pl.when(k > 1)
            def _():
                pump(k, (3, 4))

            pump(k, (5, 6, 7))

        token_wait()
        token_send()
        finish_group(k, 0)

        @pl.when(more)
        def _():
            pump_first((0, 1))
            send_edges(k + 1, 0)

        @pl.when(k > 0)
        def _():
            advance(2 * k - 1, 2)

        token_wait()
        token_send()
        finish_group(k, 1)

        @pl.when(more)
        def _():
            begin(0)
            send_edges(k + 1, 1)

        @pl.when(k > 0)
        def _():
            advance(2 * k - 1, 3)

        finish_group(k, 2)

        @pl.when(more)
        def _():
            advance(2 * k, 0)
            pump_first((2,))
            pump_later((0,))
            send_edges(k + 1, 2)

        token_wait()
        token_send()
        finish_group(k, 3)

        @pl.when(more)
        def _():
            begin(1)
            advance(2 * k, 1)
            pump_first((3,))
            pump_later((1,))
            send_edges(k + 1, 3)
            token_wait()
            token_send()
            advance(2 * k, 2)
            advance(2 * k + 1, 0)
            pump_first((4,))
            pump_later((2,))
            advance(2 * k, 3)

        return carry

    lax.fori_loop(0, DEGREE, round_of, 0)
    for g in range(groups):
        out_copy(g).start()

    def gram_part(x, acc):
        rows = jnp.concatenate(
            [
                jnp.concatenate([field[DEGREE, g, 4 + x, y] for y in range(size_y)], axis=1)
                for g in range(groups)
            ],
            axis=0,
        )
        nt = (((1,), (1,)), ((), ()))
        return acc + lax.dot_general(rows, rows, nt, preferred_element_type=F32)

    bands = groups * GROUP
    with jax.named_scope("gram_local"):
        gram = lax.fori_loop(0, size_x, gram_part, jnp.zeros((bands, bands), F32), unroll=size_x)
        gram = gram * (1.0 / float(size_x * size_y * 128 * span_x * span_y * span_z))
    packed = jnp.concatenate([gram[: bands // 2], gram[bands // 2 :]], axis=1)
    piece = bands // 2 // (span_y * span_z)
    for i in range(span_y * span_z):
        g_part[i // span_y, i % span_y] = packed[i * piece : (i + 1) * piece]

    def exchange(count, me, outgoing, landing, sends, recvs, place):
        def copy(other):
            return pltpu.make_async_remote_copy(
                outgoing(other), landing.at[me], sends.at[other], recvs.at[me], device_id=place(other)
            )

        def arrival(other):
            return pltpu.make_async_remote_copy(
                outgoing(other), landing.at[other], sends.at[other], recvs.at[other],
                device_id=place(other),
            )

        far_first = sorted(range(1, count), key=lambda d: -min(d, count - d))
        others = [lax.rem(me + d, count) for d in far_first]
        for other in others:
            copy(other).start()
        return others, copy, arrival

    def summed(landing, count):
        total = landing[0]
        for i in range(1, count):
            total = total + landing[i]
        return total

    open_sends = []

    def finish(parts):
        others, copy, arrival = parts
        for other in reversed(others):
            arrival(other).wait_recv()
        open_sends.append((others, copy))

    token_wait()
    with jax.named_scope("gram_sum"):
        at_z, at_y, at_x = here["gz"], here["gy"], here["gx"]
        run = exchange(span_z, at_z, lambda o: g_part.at[o], r_z, sz.at[0], rz.at[0], lambda o: {"gz": o})
        r_z[at_z] = g_part[at_z]
        finish(run)
        s_z[...] = summed(r_z, span_z)
        run = exchange(span_y, at_y, lambda o: s_z.at[o], r_y, sy.at[0], ry.at[0], lambda o: {"gy": o})
        r_y[at_y] = s_z[at_y]
        finish(run)
        s_y[...] = summed(r_y, span_y)
        run = exchange(span_x, at_x, lambda o: s_y, r_x, sx, rx, lambda o: {"gx": o})
        r_x[at_x] = s_y[...]
        finish(run)
        g_all[at_z, at_y] = summed(r_x, span_x)
        run = exchange(span_y, at_y, lambda o: g_all.at[at_z, at_y], g_all.at[at_z], sy.at[1], ry.at[1], lambda o: {"gy": o})
        finish(run)
        run = exchange(span_z, at_z, lambda o: g_all.at[at_z], g_all, sz.at[1], rz.at[1], lambda o: {"gz": o})
        finish(run)
        for i in range(span_y * span_z):
            line = g_all[i // span_y, i % span_y]
            gram_ref[pl.ds(i * piece, piece), :] = line[:, :bands]
            gram_ref[pl.ds(bands // 2 + i * piece, piece), :] = pltpu.roll(line, bands, 1)[:, :bands]

    def close(i, c):
        k, g = lax.div(i, groups), lax.rem(i, groups)
        for side in range(2):
            for half in range(2):
                x_copy(k, g, half, side).wait_send()
        return c

    def close_chain(chain, c):
        for stage in range(4):
            for copy in q_copies(chain, stage):
                copy.wait_send()
        return c

    with jax.named_scope("close"):
        lax.fori_loop(0, DEGREE * groups, close, 0)
        lax.fori_loop(0, 2 * (DEGREE - 1), close_chain, 0)
        for stage in range(4):
            for copy in q0_copies(stage):
                copy.wait_send()
        for others, copy in open_sends:
            for other in others:
                copy(other).wait_send()
        for g in range(groups):
            out_copy(g).wait()


def z_weights(size_z):
    coef = [-0.5 * c / FILTER_HALF for c in STENCIL]
    whole = np.zeros((2 * size_z, size_z), np.float32)
    for z in range(size_z):
        for m in range(1, 5):
            for source in (z - m, z + m):
                if source < 0:
                    at = size_z + 4 + source
                elif source >= size_z:
                    at = size_z + 4 + source - size_z
                else:
                    at = source
                whole[at, z] = coef[m]
    high = whole.astype(ml_dtypes.bfloat16)
    low = (whole - high.astype(np.float32)).astype(ml_dtypes.bfloat16)
    return np.concatenate([high, low], axis=1)


def shards(bands, potential, coupling, proj_atom, proj_cell, proj_value):
    count, size_x, size_y, size_z = bands.shape
    entries = proj_atom.shape[1]
    groups = count // GROUP
    chains = 2 * (DEGREE - 1)
    grouped = bands.reshape(groups, GROUP, size_x, size_y, size_z).transpose(0, 2, 3, 1, 4)
    vmem = pl.BlockSpec(memory_space=pltpu.VMEM)
    anywhere = pl.BlockSpec(memory_space=pl.ANY)
    dma = pltpu.SemaphoreType.DMA
    span_x, span_y, span_z = SPAN["gx"], SPAN["gy"], SPAN["gz"]
    rows = 8 * groups
    piece = count // 2 // (span_y * span_z)
    out, gram = pl.pallas_call(
        kernel,
        out_shape=(
            jax.ShapeDtypeStruct(grouped.shape, BF16),
            jax.ShapeDtypeStruct((count, count), F32),
        ),
        in_specs=[anywhere, vmem, anywhere] + [vmem] * 4,
        out_specs=(anywhere, vmem),
        scratch_shapes=[
            pltpu.VMEM((DEGREE + 1, groups, 12, size_y, GROUP, size_z), BF16),
            pltpu.VMEM((DEGREE, groups, 2, size_x, 4, GROUP, size_z), BF16),
            pltpu.VMEM((DEGREE + 1, groups, size_x, GROUP, size_z), BF16),
            pltpu.VMEM((DEGREE, groups, 2, size_x, GROUP, size_z), BF16),
            pltpu.VMEM((size_x, size_y * size_z, entries), BF16),
            pltpu.VMEM((size_x * size_y // 2, entries, 2 * size_z), BF16),
            pltpu.VMEM((entries, 2 * KEYS), BF16),
            pltpu.VMEM((2 * KEYS, entries), BF16),
            pltpu.VMEM((DEGREE, groups, 2 * GROUP, entries), BF16),
            pltpu.VMEM((coupling.size // 128, 128), F32),
            pltpu.VMEM((8, 128), F32),
            pltpu.VMEM((size_x, size_y, size_z), F32),
            pltpu.VMEM((chains, 4, rows // 2, 128), F32),
            pltpu.VMEM((chains, 4, 8, rows // 2, 128), F32),
            pltpu.VMEM((4, rows, 128), F32),
            pltpu.VMEM((4, 8, rows, 128), F32),
            pltpu.VMEM((span_z, span_y, piece, 128), F32),
            pltpu.VMEM((span_z, span_y, piece, 128), F32),
            pltpu.VMEM((span_y, piece, 128), F32),
            pltpu.VMEM((span_y, piece, 128), F32),
            pltpu.VMEM((piece, 128), F32),
            pltpu.VMEM((span_x, piece, 128), F32),
            pltpu.VMEM((span_z, span_y, piece, 128), F32),
            dma((groups + 1,)),
            dma((groups,)),
            dma((DEGREE, groups, 2, 2)),
            dma((DEGREE, groups, 2, 2)),
            dma((DEGREE, groups, 2)),
            dma((DEGREE, groups, 2)),
            dma((DEGREE, groups, 2)),
            dma((DEGREE, groups, 2)),
            dma((chains, 4, 8)),
            dma((chains, 4, 8)),
            dma((4, 8)),
            dma((4, 8)),
            dma((2, span_z)),
            dma((2, span_z)),
            dma((2, span_y)),
            dma((2, span_y)),
            dma((span_x,)),
            dma((span_x,)),
            pltpu.SemaphoreType.REGULAR((2,)),
        ],
        compiler_params=pltpu.CompilerParams(
            collective_id=0, has_side_effects=True, vmem_limit_bytes=48 * 1024 * 1024
        ),
    )(
        grouped,
        potential,
        coupling.reshape(-1, 128),
        proj_atom,
        proj_cell,
        proj_value,
        jnp.asarray(z_weights(size_z)),
    )
    filtered = out.transpose(0, 3, 1, 2, 4).reshape(bands.shape)
    return filtered, gram


def solution(mesh):
    SPAN.update(mesh.shape)
    in_specs = (
        P(None, "gx", "gy", "gz"),
        P("gx", "gy", "gz"),
        P(),
        P(("gx", "gy", "gz"), None),
        P(("gx", "gy", "gz"), None),
        P(("gx", "gy", "gz"), None),
    )
    out_specs = (P(None, "gx", "gy", "gz"), P())
    return jax.shard_map(shards, mesh=mesh, in_specs=in_specs, out_specs=out_specs, check_vma=False)
```
